32 devices in a mesh: row: 8 (over z, core), col: 4 (over y, x).
Axes of the slice: x: 2, y: 2, z: 4, core: 2. Of those that a mesh axis runs over, the one named last changes fastest.
Arguments:
- loads: float32 [48, 1024, 4096], P(None, 'row', 'col'), may hold values from -6 to 6
- below_first: float32 [47, 1024, 1024], P(None, 'row', 'col'), may hold values from -0.1875 to 0.1875
- below_second: float32 [46, 1024, 1024], P(None, 'row', 'col'), may hold values from -0.1875 to 0.1875
- inverses: float32 [2, 1024, 1024], P(None, None, 'row'), may hold values from -1 to 2, as said below
Outputs:
- solved: float32 [2, 1024, 4096], P(None, None, 'col')
- remaining: float32 [46, 1024, 4096], P(None, 'row', 'col')
The draws below stay inside these ranges and needn't reach their ends.
Inputs may be any that keep to these rules, and one draw needn't show every extreme that they name: `inverses`: each of the two matrices is lower triangular, with a diagonal from 0.5 to 2.
All inputs are finite; a program needn't handle non-finite values.
Results may differ from the reference program's by a relative error of at most 0.000084.
Values sent between devices are 32-bit elements; how exact they have to be, the bound alone decides.
A program may use at most 256 MiB of HBM per device.

```python
import math
import jax
import jax.numpy as jnp
from jax import lax

NB = 1024
CYC = 48
NRHS = 4096


def draw_inverses(key, part):
    key_entries = jax.random.fold_in(key, 11)
    key_diagonal = jax.random.fold_in(key, 12)
    row_index = lax.broadcasted_iota(jnp.int32, (2, NB, NB), 1)
    col_index = lax.broadcasted_iota(jnp.int32, (2, NB, NB), 2)
    entries = jax.random.normal(key_entries, (2, NB, NB), jnp.float32)
    diagonal_vals = jax.random.uniform(key_diagonal, (2, NB, NB), jnp.float32, 0.5, 2.0)
    scaled = entries / math.sqrt(NB)
    triangle = jnp.where(col_index < row_index, scaled, jnp.where(col_index == row_index, diagonal_vals, 0.0))
    return triangle.astype(jnp.float32)


def level_of(rng, dims, pieces, smallest, high):
    loudness, own = 1.0, jax.random.fold_in(rng, 6)
    for axis_at, shards_of in pieces:
        heights = jnp.exp(jax.random.uniform(jax.random.fold_in(own, axis_at), (shards_of,), jnp.float32, smallest / len(pieces), high / len(pieces)))
        loudness = loudness * jnp.repeat(heights, dims[axis_at] // shards_of).reshape([-1 if axis == axis_at else 1 for axis in range(len(dims))])
    return loudness


def bell_draw(rng, dims, scale, limit, split=(), kind=jnp.bfloat16):
    result = jax.random.normal(rng, dims, jnp.float32) * scale
    if len(split) > 0:
        result = level_of(rng, dims, split, -0.22, 0.18) * result
    return jnp.clip(result, min=-limit, max=limit).astype(kind)


def setup_inputs(seed: int = 0) -> dict:
    keys = jax.random.split(jax.random.key(seed), 5)
    return {
        "loads": bell_draw(keys[0], (CYC, NB, NRHS), 1.0, 6.0, ((1, 8), (2, 4)), jnp.float32),
        "below_first": bell_draw(keys[1], (CYC - 1, NB, NB), NB ** -0.5, 0.1875, ((1, 8), (2, 4)), jnp.float32),
        "below_second": bell_draw(keys[2], (CYC - 2, NB, NB), NB ** -0.5, 0.1875, ((1, 8), (2, 4)), jnp.float32),
        "inverses": draw_inverses(jax.random.fold_in(keys[4], 71), 0),
    }


def reference(loads, below_first, below_second, inverses):
    highest = lax.Precision.HIGHEST
    first_block = jnp.dot(inverses[0], loads[0], precision=highest)
    product_one = jnp.dot(below_first.reshape(-1, NB), first_block, precision=highest)
    updated = loads[1:] - product_one.reshape(CYC - 1, NB, NRHS)
    second_block = jnp.dot(inverses[1], updated[0], precision=highest)
    product_two = jnp.dot(below_second.reshape(-1, NB), second_block, precision=highest)
    remaining = updated[1:] - product_two.reshape(CYC - 2, NB, NRHS)
    return jnp.stack([first_block, second_block]), remaining
```

```python
import functools
import jax
import jax.numpy as jnp
from jax import lax
from jax.experimental import pallas as pl
from jax.experimental.pallas import tpu as pltpu
from jax.sharding import PartitionSpec as P

HIGH = lax.Precision.HIGH
MESH = pl.DeviceIdType.MESH
STEPS = 4


def chunk_sizes(count):
    sizes = []
    for size in (8, 4, 2):
        while count - size >= size // 2:
            sizes.append(size)
            count -= size
    return sizes + [count] if count else sizes


def halves(value):
    high = value.astype(jnp.bfloat16)
    return high, (value - high.astype(jnp.float32)).astype(jnp.bfloat16)


def product(x, y):
    dot = functools.partial(jnp.dot, preferred_element_type=jnp.float32)
    return dot(x[0], y[0]) + dot(x[0], y[1]) + dot(x[1], y[0])


def solve_kernel(sizes, loads, first, second, inverses, *refs):
    count = len(sizes)
    solved, (high, low, x1, y2, d1, d2) = refs[:2], refs[2:8]
    x2, y1 = refs[8:8 + count], refs[8 + count:8 + 2 * count]
    (inv, rhs, top, part, swapped, passed, block, high_stage, low_stage,
     local_sem, link_send, link_recv, sum_send, sum_recv) = refs[8 + 2 * count:]
    r, c = lax.axis_index("row"), lax.axis_index("col")
    z, core = r // 2, lax.rem(r, 2)
    chips = inv.shape[1] // inv.shape[2] // 2
    rows = inv.shape[2]
    width = first.shape[2]
    x_side = c + 1 - 2 * lax.rem(c, 2)
    y_side = lax.rem(c + 2, 4)
    x_to, y_to = (r, x_side), (r, y_side)
    core_to = (r + 1 - 2 * core, c)

    def z_place(d):
        return lax.rem(z + d + chips, chips)

    def z_to(d):
        return (z_place(d) * 2 + core, c)

    def remote(src, dst, sends, recvs, at, to):
        return pltpu.make_async_remote_copy(src, dst, sends.at[at], recvs.at[at], device_id=to, device_id_type=MESH)

    inv_in = pltpu.make_async_copy(inverses, inv, local_sem.at[0])
    rhs_in = pltpu.make_async_copy(loads.at[pl.ds(0, 2)], rhs, local_sem.at[1])
    top_in = pltpu.make_async_copy(first.at[0], top.at[c], local_sem.at[2])
    inv_in.start()
    rhs_in.start()
    top_in.start()

    barrier = pltpu.get_barrier_semaphore()
    partners = [x_to, y_to, core_to] + [z_to(d) for d in range(1, chips)]
    for to in partners:
        pl.semaphore_signal(barrier, inc=1, device_id=to, device_id_type=MESH)
    pl.semaphore_wait(barrier, len(partners))

    top_in.wait()
    link = functools.partial(remote, sends=link_send, recvs=link_recv)
    top_x = link(top.at[c], top.at[c], at=0, to=x_to)
    top_y = link(top.at[c], top.at[c], at=1, to=y_to)
    top_d = link(top.at[y_side], top.at[y_side], at=2, to=x_to)
    total_blocks = sum(sizes)
    send_x1 = link(first.at[pl.ds(1, total_blocks)], x1, at=3, to=x_to)
    send_y2 = link(second, y2, at=4, to=y_to)
    send_d1 = link(y1[0], d1, at=5, to=x_to)
    send_d2 = link(x2[0], d2, at=6, to=y_to)
    send_x2, send_y1 = [], []
    start = 0
    for k, size in enumerate(sizes):
        send_x2.append(link(second.at[pl.ds(start, size)], x2[k], at=7 + k, to=x_to))
        send_y1.append(link(first.at[pl.ds(start + 1, size)], y1[k], at=7 + count + k, to=y_to))
        start += size
    for copy in (top_x, top_y, send_x2[0], send_y1[0]):
        copy.start()

    def top_recv(q, at):
        link(top.at[q], top.at[q], at=at, to=x_to).wait_recv()

    def finish(j, before, between):
        base = j * (4 * chips)
        at = functools.partial(remote, sends=sum_send, recvs=sum_recv)
        away = at(part.at[j, pl.ds((1 - core) * chips, chips)], swapped.at[j], at=base, to=core_to)
        away.start()
        before()
        away.wait_recv()

        @pl.loop(0, chips)
        def _(i):
            part[j, core * chips + i] += swapped[j, i]

        out = []
        for d in range(1, chips):
            copy = at(part.at[j, core * chips + z_place(d)], passed.at[j, d - 1], at=base + d, to=z_to(d))
            copy.start()
            out.append(copy)
        between()
        for copy in out:
            copy.wait_recv()
        mine = pl.ds(pl.multiple_of(r * rows, rows), rows)
        total = part[j, core * chips + z]
        for d in range(1, chips):
            total = total + passed[j, d - 1]
        block[j, mine] = total
        gathered = []
        for d in range(1, chips):
            copy = at(block.at[j, mine], block.at[j, mine], at=base + chips - 1 + d, to=z_to(d))
            copy.start()
            gathered.append(copy)
        across = [at(block.at[j, mine], block.at[j, mine], at=base + 2 * chips - 1, to=core_to)]
        across[0].start()
        return away, out, gathered, across, base, at

    def complete(j, state):
        away, out, gathered, across, base, at = state
        for d in range(1, chips):
            here = pl.ds(pl.multiple_of((z_place(-d) * 2 + core) * rows, rows), rows)
            at(block.at[j, here], block.at[j, here], at=base + chips - 1 + d, to=z_to(d)).wait_recv()
            copy = at(block.at[j, here], block.at[j, here], at=base + 2 * chips - 1 + d, to=core_to)
            copy.start()
            across.append(copy)
        for d in range(chips):
            there = pl.ds(pl.multiple_of((z_place(-d) * 2 + 1 - core) * rows, rows), rows)
            at(block.at[j, there], block.at[j, there], at=base + 2 * chips - 1 + d, to=core_to).wait_recv()
        for copy in [away] + out + gathered + across:
            copy.wait_send()

    def term(j, right):
        @pl.loop(0, 2 * chips)
        def _(i):
            owner = lax.rem(i, chips) * 2 + i // chips
            left = inv[j, pl.ds(pl.multiple_of(owner * rows, rows), rows)]
            part[j, i] = product(halves(left), right)

    def stage(j):
        for k, q in enumerate((c, x_side, y_side, 3 - c)):
            quarter = block[j, pl.ds(pl.multiple_of(q * width, width), width)]
            h, l = halves(quarter)
            high_stage[j, k * width:(k + 1) * width] = h
            low_stage[j, k * width:(k + 1) * width] = l
        depth = 4 * width
        copies = [
            pltpu.make_async_copy(block.at[j], solved[j], local_sem.at[3 + 3 * j]),
            pltpu.make_async_copy(high_stage.at[j], high.at[pl.ds(j * depth, depth)], local_sem.at[4 + 3 * j]),
            pltpu.make_async_copy(low_stage.at[j], low.at[pl.ds(j * depth, depth)], local_sem.at[5 + 3 * j]),
        ]
        for copy in copies:
            copy.start()
        return copies

    inv_in.wait()
    rhs_in.wait()
    term(0, halves(rhs[0]))

    def forward_top():
        top_recv(y_side, 1)
        top_d.start()
        for copy in send_x2[1:] + send_y1[1:]:
            copy.start()

    def queue_rest():
        send_x1.start()
        send_y2.start()

    def forward_first():
        send_y1[0].wait_recv()
        send_d1.start()
        send_x2[0].wait_recv()
        send_d2.start()

    def nothing():
        pass

    state = finish(0, forward_top, queue_rest)
    complete(0, state)
    copies = stage(0)
    top_recv(x_side, 0)
    top_recv(3 - c, 2)
    update = rhs[1]
    for q in range(4):
        left = halves(top[q])
        right = halves(block[0, q * width:(q + 1) * width])
        update = update - product(left, right)
    term(1, halves(update))

    state = finish(1, nothing, forward_first)
    complete(1, state)
    copies += stage(1)
    for copy in copies:
        copy.wait()
    for copy in (top_x, top_y, top_d):
        copy.wait_send()
    for copy in [send_x1, send_y2, send_d1, send_d2] + send_x2[1:] + send_y1[1:]:
        copy.wait()
    for copy in (send_x2[0], send_y1[0]):
        copy.wait_send()


def solve(sizes, row_count, loads, first, second, inverses):
    chips = row_count // 2
    rows, columns = loads.shape[1:]
    width = first.shape[2]
    depth = 4 * width
    f32, bf16 = jnp.float32, jnp.bfloat16
    anywhere = pl.BlockSpec(memory_space=pl.ANY)
    shape = jax.ShapeDtypeStruct
    piece = lambda size: shape((size, rows, width), f32)
    pieces = [piece(size) for size in [sum(sizes)] * 2 + [sizes[0]] * 2 + list(sizes) * 2]
    links = 7 + 2 * len(sizes)
    sums = 2 * 4 * chips
    return pl.pallas_call(
        functools.partial(solve_kernel, sizes),
        out_shape=[shape((depth, columns), f32)] * 2 + [shape((2 * depth, columns), bf16)] * 2 + pieces,
        in_specs=[anywhere] * 4,
        out_specs=[anywhere] * (4 + len(pieces)),
        scratch_shapes=[
            pltpu.VMEM((2, depth, rows), f32),
            pltpu.VMEM((2, rows, columns), f32),
            pltpu.VMEM((4, rows, width), f32),
            pltpu.VMEM((2, 2 * chips, rows, columns), f32),
            pltpu.VMEM((2, chips, rows, columns), f32),
            pltpu.VMEM((2, chips - 1, rows, columns), f32),
            pltpu.VMEM((2, depth, columns), f32),
            pltpu.VMEM((2, depth, columns), bf16),
            pltpu.VMEM((2, depth, columns), bf16),
            pltpu.SemaphoreType.DMA((9,)),
            pltpu.SemaphoreType.DMA((links,)),
            pltpu.SemaphoreType.DMA((links,)),
            pltpu.SemaphoreType.DMA((sums,)),
            pltpu.SemaphoreType.DMA((sums,)),
        ],
        compiler_params=pltpu.CompilerParams(
            collective_id=0, has_side_effects=True, vmem_limit_bytes=60 * 1024 * 1024,
        ),
    )(loads, first, second, inverses)


def update_kernel(count, step, *refs):
    pieces = refs[:count]
    loads = refs[count:count + step // 2]
    high_ref, low_ref = refs[count + step // 2:count + step // 2 + 2]
    out, ah, al = refs[-3:]
    rows, width = pieces[0].shape[1:]
    for at, piece in enumerate(pieces):
        high, low = halves(piece[...].reshape(step * rows, width))
        ah[:, at * width:(at + 1) * width] = high
        al[:, at * width:(at + 1) * width] = low
    total = product((ah[...], al[...]), (high_ref[...], low_ref[...]))
    total = total.reshape(step, rows, total.shape[1])
    for at, part in enumerate(loads):
        out[2 * at:2 * at + 2] = part[...] - total[2 * at:2 * at + 2]


def update_chunk(firsts, seconds, loads, high, low, offset, size, previous):
    rows, width = firsts[0][0].shape[1:]
    columns = loads.shape[2]
    depth = high.shape[0]
    count = loads.shape[0] - 2
    step = STEPS if size % STEPS == 0 and offset % STEPS == 0 else 2
    operands, in_specs = [], []
    for array, at in firsts + seconds:
        operands.append(array)
        in_specs.append(pl.BlockSpec(
            (pl.Element(step), pl.Element(rows), pl.Element(width)),
            lambda i, at=at: (at + i * step, 0, 0)))
    for k in range(step // 2):
        operands.append(loads)
        in_specs.append(pl.BlockSpec((2, rows, columns), lambda i, k=k: (1 + (offset + i * step) // 2 + k, 0, 0)))
    for factor in (high, low):
        operands.append(factor)
        in_specs.append(pl.BlockSpec((depth, columns), lambda i: (0, 0), pipeline_mode=pl.Buffered(1)))
    aliases = {}
    if previous is not None:
        aliases = {len(operands): 0}
        operands.append(previous)
        in_specs.append(pl.BlockSpec(memory_space=pl.ANY))
    work = size * rows * depth * columns
    return pl.pallas_call(
        functools.partial(update_kernel, len(firsts + seconds), step),
        out_shape=jax.ShapeDtypeStruct((count, rows, columns), jnp.float32),
        grid=(size // step,),
        in_specs=in_specs,
        out_specs=pl.BlockSpec((step, rows, columns), lambda i: (offset // step + i, 0, 0)),
        scratch_shapes=[pltpu.VMEM((step * rows, depth), jnp.bfloat16)] * 2,
        input_output_aliases=aliases,
        compiler_params=pltpu.CompilerParams(vmem_limit_bytes=60 * 1024 * 1024),
        cost_estimate=pl.CostEstimate(
            flops=6 * work,
            bytes_accessed=4 * size * rows * (depth + 2 * columns) + 4 * depth * columns,
            transcendentals=0,
        ),
    )(*operands)


def local_quarters(row_count, loads, below_first, below_second, inverses):
    sizes = chunk_sizes(loads.shape[0] - 2)
    along_x = [(c, c ^ 1) for c in range(4)]
    along_y = [(c, c ^ 2) for c in range(4)]
    results = solve(sizes, row_count, loads, below_first, below_second, inverses)
    solved, (high, low, x1, y2, d1, d2) = results[:2], results[2:8]
    x2, y1 = results[8:8 + len(sizes)], results[8 + len(sizes):]
    solved, high = lax.optimization_barrier((jnp.stack(solved), high))
    d1 = [d1] + [lax.ppermute(piece, "col", along_x) for piece in y1[1:]]
    d2 = [d2] + [lax.ppermute(piece, "col", along_y) for piece in x2[1:]]
    remaining = None
    at = 0
    for k, size in enumerate(sizes):
        firsts = [(below_first, at + 1), (x1, at), (y1[k], 0), (d1[k], 0)]
        seconds = [(below_second, at), (x2[k], 0), (y2, at), (d2[k], 0)]
        remaining = update_chunk(firsts, seconds, loads, high, low, at, size, remaining)
        at += size
    return solved, remaining


def local_gathered(loads, below_first, below_second, inverses):
    count = loads.shape[0] - 2
    gather = lambda piece: lax.all_gather(piece, "col", axis=2, tiled=True)
    top = gather(below_first[:1])
    first_block = lax.psum(jnp.dot(inverses[0], loads[0], precision=HIGH), "row")
    updated = loads[1] - jnp.dot(top[0], first_block, precision=HIGH)
    second_block = lax.psum(jnp.dot(inverses[1], updated, precision=HIGH), "row")
    solved = jnp.stack([first_block, second_block])
    whole = solved.reshape(-1, solved.shape[2])
    high = lax.reduce_precision(whole, 8, 7)
    high, low = high.astype(jnp.bfloat16), (whole - high).astype(jnp.bfloat16)
    remaining = None
    at = 0
    for size in (count // 8 * 4, count - count // 8 * 4):
        firsts = [(gather(below_first[at + 1:at + 1 + size]), 0)]
        seconds = [(gather(below_second[at:at + size]), 0)]
        remaining = update_chunk(firsts, seconds, loads, high, low, at, size, remaining)
        at += size
    return solved, remaining


def solution(mesh):
    in_specs = (
        P(None, "row", "col"),
        P(None, "row", "col"),
        P(None, "row", "col"),
        P(None, None, "row"),
    )
    out_specs = (P(None, None, "col"), P(None, "row", "col"))
    quarters = mesh.shape["col"] == 4 and mesh.shape["row"] % 2 == 0
    local = functools.partial(local_quarters, mesh.shape["row"]) if quarters else local_gathered
    return jax.shard_map(local, mesh=mesh, in_specs=in_specs, out_specs=out_specs, check_vma=False)
```

```python
import functools
import jax
import jax.numpy as jnp
from jax import lax
from jax.experimental import pallas as pl
from jax.experimental.pallas import tpu as pltpu
from jax.sharding import PartitionSpec as P

HIGH = lax.Precision.HIGH
MESH = pl.DeviceIdType.MESH
STEP = 2
STEPS = 4


def chunk_sizes(count):
    sizes = []
    for size in (8, 4, 2):
        while count - size >= size // 2:
            sizes.append(size)
            count -= size
    return sizes + [count] if count else sizes


def halves(value):
    high = value.astype(jnp.bfloat16)
    return high, (value - high.astype(jnp.float32)).astype(jnp.bfloat16)


def product(x, y):
    dot = functools.partial(jnp.dot, preferred_element_type=jnp.float32)
    return dot(x[0], y[0]) + dot(x[0], y[1]) + dot(x[1], y[0])


def solve_kernel(sizes, loads, first, second, inverses, *refs):
    count = len(sizes)
    solved, (high, low, partial, x1, y2, d1, d2) = refs[:2], refs[2:9]
    x2, y1 = refs[9:9 + count], refs[9 + count:9 + 2 * count]
    (inv, rhs, top, part, swapped, passed, block, high_stage, low_stage,
     split_high, split_low,
     local_sem, link_send, link_recv, sum_send, sum_recv) = refs[9 + 2 * count:]
    r, c = lax.axis_index("row"), lax.axis_index("col")
    z, core = r // 2, lax.rem(r, 2)
    chips = inv.shape[1] // inv.shape[2] // 2
    rows = inv.shape[2]
    width = first.shape[2]
    x_side = c + 1 - 2 * lax.rem(c, 2)
    y_side = lax.rem(c + 2, 4)
    x_to, y_to = (r, x_side), (r, y_side)
    core_to = (r + 1 - 2 * core, c)

    def z_place(d):
        return lax.rem(z + d + chips, chips)

    def z_to(d):
        return (z_place(d) * 2 + core, c)

    def remote(src, dst, sends, recvs, at, to):
        return pltpu.make_async_remote_copy(src, dst, sends.at[at], recvs.at[at], device_id=to, device_id_type=MESH)

    inv_in = pltpu.make_async_copy(inverses, inv, local_sem.at[0])
    rhs_in = pltpu.make_async_copy(loads.at[pl.ds(0, 2)], rhs, local_sem.at[1])
    top_in = pltpu.make_async_copy(first.at[0], top.at[c], local_sem.at[2])
    inv_in.start()
    rhs_in.start()
    top_in.start()

    barrier = pltpu.get_barrier_semaphore()
    partners = [x_to, y_to, core_to] + [z_to(d) for d in range(1, chips)]
    for to in partners:
        pl.semaphore_signal(barrier, inc=1, device_id=to, device_id_type=MESH)
    pl.semaphore_wait(barrier, len(partners))

    top_in.wait()
    link = functools.partial(remote, sends=link_send, recvs=link_recv)
    top_x = link(top.at[c], top.at[c], at=0, to=x_to)
    top_y = link(top.at[c], top.at[c], at=1, to=y_to)
    top_d = link(top.at[y_side], top.at[y_side], at=2, to=x_to)
    send_d1 = link(y1[0], d1, at=3, to=x_to)
    send_d2 = link(x2[0], d2, at=4, to=y_to)
    starts = [sum(sizes[:k]) for k in range(count)]
    owned, send_x2, send_y1, send_x1, send_y2 = [], [], [], [], []
    for k, (start, size) in enumerate(zip(starts, sizes)):
        own1, own2 = first.at[pl.ds(start + 1, size)], second.at[pl.ds(start, size)]
        owned.append((own1, own2))
        send_x2.append(link(own2, x2[k], at=5 + 4 * k, to=x_to))
        send_y1.append(link(own1, y1[k], at=6 + 4 * k, to=y_to))
        send_x1.append(link(own1, x1.at[pl.ds(start, size)], at=7 + 4 * k, to=x_to))
        send_y2.append(link(own2, y2.at[pl.ds(start, size)], at=8 + 4 * k, to=y_to))
    for copy in (top_x, top_y, send_x2[0], send_y1[0]):
        copy.start()

    def top_recv(q, at):
        link(top.at[q], top.at[q], at=at, to=x_to).wait_recv()

    def finish(j, before, between):
        base = j * (4 * chips)
        at = functools.partial(remote, sends=sum_send, recvs=sum_recv)
        away = at(part.at[j, pl.ds((1 - core) * chips, chips)], swapped.at[j], at=base, to=core_to)
        away.start()
        before()
        away.wait_recv()

        @pl.loop(0, chips)
        def _(i):
            part[j, core * chips + i] += swapped[j, i]

        out = []
        for d in range(1, chips):
            copy = at(part.at[j, core * chips + z_place(d)], passed.at[j, d - 1], at=base + d, to=z_to(d))
            copy.start()
            out.append(copy)
        between()
        for copy in out:
            copy.wait_recv()
        mine = pl.ds(pl.multiple_of(r * rows, rows), rows)
        total = part[j, core * chips + z]
        for d in range(1, chips):
            total = total + passed[j, d - 1]
        block[j, mine] = total
        gathered = []
        for d in range(1, chips):
            copy = at(block.at[j, mine], block.at[j, mine], at=base + chips - 1 + d, to=z_to(d))
            copy.start()
            gathered.append(copy)
        across = [at(block.at[j, mine], block.at[j, mine], at=base + 2 * chips - 1, to=core_to)]
        across[0].start()
        return away, out, gathered, across, base, at

    def complete(j, state):
        away, out, gathered, across, base, at = state
        for d in range(1, chips):
            here = pl.ds(pl.multiple_of((z_place(-d) * 2 + core) * rows, rows), rows)
            at(block.at[j, here], block.at[j, here], at=base + chips - 1 + d, to=z_to(d)).wait_recv()
            copy = at(block.at[j, here], block.at[j, here], at=base + 2 * chips - 1 + d, to=core_to)
            copy.start()
            across.append(copy)
        for d in range(chips):
            there = pl.ds(pl.multiple_of((z_place(-d) * 2 + 1 - core) * rows, rows), rows)
            at(block.at[j, there], block.at[j, there], at=base + 2 * chips - 1 + d, to=core_to).wait_recv()
        for copy in [away] + out + gathered + across:
            copy.wait_send()

    def term(j, right):
        @pl.loop(0, 2 * chips)
        def _(i):
            owner = lax.rem(i, chips) * 2 + i // chips
            left = inv[j, pl.ds(pl.multiple_of(owner * rows, rows), rows)]
            part[j, i] = product(halves(left), right)

    def stage(j):
        for k, q in enumerate((c, x_side, y_side, 3 - c)):
            quarter = block[j, pl.ds(pl.multiple_of(q * width, width), width)]
            h, l = halves(quarter)
            high_stage[j, k * width:(k + 1) * width] = h
            low_stage[j, k * width:(k + 1) * width] = l
        near, here = 3 * width, pl.ds(j * width, width)
        copies = [
            pltpu.make_async_copy(block.at[j], solved[j], local_sem.at[3 + 3 * j]),
            pltpu.make_async_copy(high_stage.at[j, pl.ds(near, width)], high.at[here], local_sem.at[4 + 3 * j]),
            pltpu.make_async_copy(low_stage.at[j, pl.ds(near, width)], low.at[here], local_sem.at[5 + 3 * j]),
        ]
        for copy in copies:
            copy.start()
        return copies

    inv_in.wait()
    rhs_in.wait()
    term(0, halves(rhs[0]))

    def forward_top():
        top_recv(y_side, 1)
        top_d.start()
        send_x1[0].start()
        send_y2[0].start()

    def queue_rest():
        for k in range(1, count):
            for copy in (send_x2[k], send_y1[k], send_x1[k], send_y2[k]):
                copy.start()

    def forward_first():
        send_y1[0].wait_recv()
        send_d1.start()
        send_x2[0].wait_recv()
        send_d2.start()

    def nothing():
        pass

    state = finish(0, forward_top, queue_rest)
    complete(0, state)
    copies = stage(0)
    top_recv(x_side, 0)
    top_recv(3 - c, 2)
    update = rhs[1]
    for q in range(4):
        left = halves(top[q])
        right = halves(block[0, q * width:(q + 1) * width])
        update = update - product(left, right)
    term(1, halves(update))

    state = finish(1, nothing, forward_first)
    complete(1, state)
    copies += stage(1)

    near = 3 * width

    def step_body(*views):
        loads_view, out_view = views[6:]
        for at, piece in enumerate(views[:6]):
            h, l = halves(piece[...].reshape(STEP * rows, width))
            split_high[:, at * width:(at + 1) * width] = h
            split_low[:, at * width:(at + 1) * width] = l
        total = product((split_high[:, :near], split_low[:, :near]), (high_stage[0, :near], low_stage[0, :near]))
        total = total + product((split_high[:, near:], split_low[:, near:]), (high_stage[1, :near], low_stage[1, :near]))
        out_view[...] = loads_view[...] - total.reshape(STEP, rows, total.shape[1])

    columns = rhs.shape[2]
    narrow = pl.BlockSpec((STEP, rows, width), lambda i: (i, 0, 0))
    wide = pl.BlockSpec((STEP, rows, columns), lambda i: (i, 0, 0))
    for k, (start, size) in enumerate(zip(starts, sizes)):
        here = pl.ds(start, size)
        for copy in (send_x1[k], send_y2[k]) + ((send_x2[k], send_y1[k]) if k else ()):
            copy.wait_recv()
        pltpu.emit_pipeline(step_body, grid=(size // STEP,), in_specs=[narrow] * 6 + [wide], out_specs=[wide])(
            owned[k][0], x1.at[here], y1[k], owned[k][1], x2[k], y2.at[here],
            loads.at[pl.ds(start + 2, size)], partial.at[here])
    for copy in copies:
        copy.wait()
    for copy in [top_x, top_y, top_d] + send_x1 + send_y1 + send_x2 + send_y2:
        copy.wait_send()
    for copy in (send_d1, send_d2):
        copy.wait()


def solve(sizes, row_count, loads, first, second, inverses):
    chips = row_count // 2
    rows, columns = loads.shape[1:]
    width = first.shape[2]
    depth = 4 * width
    f32, bf16 = jnp.float32, jnp.bfloat16
    anywhere = pl.BlockSpec(memory_space=pl.ANY)
    shape = jax.ShapeDtypeStruct
    piece = lambda size: shape((size, rows, width), f32)
    pieces = [piece(size) for size in [sum(sizes)] * 2 + [sizes[0]] * 2 + list(sizes) * 2]
    links = 5 + 4 * len(sizes)
    sums = 2 * 4 * chips
    return pl.pallas_call(
        functools.partial(solve_kernel, sizes),
        out_shape=[shape((depth, columns), f32)] * 2 + [shape((2 * width, columns), bf16)] * 2
        + [shape((sum(sizes), rows, columns), f32)] + pieces,
        in_specs=[anywhere] * 4,
        out_specs=[anywhere] * (5 + len(pieces)),
        scratch_shapes=[
            pltpu.VMEM((2, depth, rows), f32),
            pltpu.VMEM((2, rows, columns), f32),
            pltpu.VMEM((4, rows, width), f32),
            pltpu.VMEM((2, 2 * chips, rows, columns), f32),
            pltpu.VMEM((2, chips, rows, columns), f32),
            pltpu.VMEM((2, chips - 1, rows, columns), f32),
            pltpu.VMEM((2, depth, columns), f32),
            pltpu.VMEM((2, depth, columns), bf16),
            pltpu.VMEM((2, depth, columns), bf16),
            pltpu.VMEM((STEP * rows, 6 * width), bf16),
            pltpu.VMEM((STEP * rows, 6 * width), bf16),
            pltpu.SemaphoreType.DMA((9,)),
            pltpu.SemaphoreType.DMA((links,)),
            pltpu.SemaphoreType.DMA((links,)),
            pltpu.SemaphoreType.DMA((sums,)),
            pltpu.SemaphoreType.DMA((sums,)),
        ],
        compiler_params=pltpu.CompilerParams(
            collective_id=0, has_side_effects=True, vmem_limit_bytes=60 * 1024 * 1024,
        ),
    )(loads, first, second, inverses)


def update_kernel(count, step, *refs):
    pieces = refs[:count]
    loads = refs[count:count + step // 2]
    high_ref, low_ref = refs[count + step // 2:count + step // 2 + 2]
    out, ah, al = refs[-3:]
    rows, width = pieces[0].shape[1:]
    for at, piece in enumerate(pieces):
        high, low = halves(piece[...].reshape(step * rows, width))
        ah[:, at * width:(at + 1) * width] = high
        al[:, at * width:(at + 1) * width] = low
    total = product((ah[...], al[...]), (high_ref[...], low_ref[...]))
    total = total.reshape(step, rows, total.shape[1])
    for at, part in enumerate(loads):
        out[2 * at:2 * at + 2] = part[...] - total[2 * at:2 * at + 2]


def update_chunk(pieces, loads, skip, high, low, offset, size, previous):
    rows, width = pieces[0].shape[1:]
    columns = loads.shape[2]
    depth = high.shape[0]
    count = loads.shape[0] - skip
    step = STEPS if size % STEPS == 0 and offset % STEPS == 0 else 2
    operands, in_specs = [], []
    for array in pieces:
        operands.append(array)
        in_specs.append(pl.BlockSpec((step, rows, width), lambda i: (i, 0, 0)))
    for k in range(step // 2):
        operands.append(loads)
        in_specs.append(pl.BlockSpec((2, rows, columns), lambda i, k=k: ((skip + offset + i * step) // 2 + k, 0, 0)))
    for factor in (high, low):
        operands.append(factor)
        in_specs.append(pl.BlockSpec((depth, columns), lambda i: (0, 0), pipeline_mode=pl.Buffered(1)))
    aliases = {}
    if previous is not None:
        aliases = {len(operands): 0}
        operands.append(previous)
        in_specs.append(pl.BlockSpec(memory_space=pl.ANY))
    work = size * rows * depth * columns
    return pl.pallas_call(
        functools.partial(update_kernel, len(pieces), step),
        out_shape=jax.ShapeDtypeStruct((count, rows, columns), jnp.float32),
        grid=(size // step,),
        in_specs=in_specs,
        out_specs=pl.BlockSpec((step, rows, columns), lambda i: (offset // step + i, 0, 0)),
        scratch_shapes=[pltpu.VMEM((step * rows, depth), jnp.bfloat16)] * 2,
        input_output_aliases=aliases,
        compiler_params=pltpu.CompilerParams(vmem_limit_bytes=60 * 1024 * 1024),
        cost_estimate=pl.CostEstimate(
            flops=6 * work,
            bytes_accessed=4 * size * rows * (depth + 2 * columns) + 4 * depth * columns,
            transcendentals=0,
        ),
    )(*operands)


def local_quarters(row_count, loads, below_first, below_second, inverses):
    sizes = chunk_sizes(loads.shape[0] - 2)
    along_x = [(c, c ^ 1) for c in range(4)]
    along_y = [(c, c ^ 2) for c in range(4)]
    results = solve(sizes, row_count, loads, below_first, below_second, inverses)
    solved, (high, low, partial, x1, y2, d1, d2) = results[:2], results[2:9]
    x2, y1 = results[9:9 + len(sizes)], results[9 + len(sizes):]
    solved, high = lax.optimization_barrier((jnp.stack(solved), high))
    d1 = [d1] + [lax.ppermute(piece, "col", along_x) for piece in y1[1:]]
    d2 = [d2] + [lax.ppermute(piece, "col", along_y) for piece in x2[1:]]
    remaining = None
    at = 0
    for k, size in enumerate(sizes):
        remaining = update_chunk([d1[k], d2[k]], partial, 0, high, low, at, size, remaining)
        at += size
    return solved, remaining


def local_gathered(loads, below_first, below_second, inverses):
    count = loads.shape[0] - 2
    gather = lambda piece: lax.all_gather(piece, "col", axis=2, tiled=True)
    top = gather(below_first[:1])
    first_block = lax.psum(jnp.dot(inverses[0], loads[0], precision=HIGH), "row")
    updated = loads[1] - jnp.dot(top[0], first_block, precision=HIGH)
    second_block = lax.psum(jnp.dot(inverses[1], updated, precision=HIGH), "row")
    solved = jnp.stack([first_block, second_block])
    whole = solved.reshape(-1, solved.shape[2])
    high = lax.reduce_precision(whole, 8, 7)
    high, low = high.astype(jnp.bfloat16), (whole - high).astype(jnp.bfloat16)
    remaining = None
    at = 0
    for size in (count // 8 * 4, count - count // 8 * 4):
        pieces = [gather(below_first[at + 1:at + 1 + size]), gather(below_second[at:at + size])]
        remaining = update_chunk(pieces, loads, 2, high, low, at, size, remaining)
        at += size
    return solved, remaining


def solution(mesh):
    in_specs = (
        P(None, "row", "col"),
        P(None, "row", "col"),
        P(None, "row", "col"),
        P(None, None, "row"),
    )
    out_specs = (P(None, None, "col"), P(None, "row", "col"))
    quarters = mesh.shape["col"] == 4 and mesh.shape["row"] % 2 == 0
    local = functools.partial(local_quarters, mesh.shape["row"]) if quarters else local_gathered
    return jax.shard_map(local, mesh=mesh, in_specs=in_specs, out_specs=out_specs, check_vma=False)
```

```python
import functools
import jax
import jax.numpy as jnp
from jax import lax
from jax.experimental import pallas as pl
from jax.experimental.pallas import tpu as pltpu
from jax.sharding import PartitionSpec as P

HIGH = lax.Precision.HIGH
MESH = pl.DeviceIdType.MESH
STEP = 2
STEPS = 4


def chunk_sizes(count):
    first, last = count // 10 * 2, count // 20 * 2
    middle = count - first - last
    parts = -(-middle // 12)
    at = [k * middle // (2 * parts) * 2 for k in range(parts)] + [middle]
    return [first] + [after - before for before, after in zip(at, at[1:])] + [last]


def halves(value):
    high = value.astype(jnp.bfloat16)
    return high, (value - high.astype(jnp.float32)).astype(jnp.bfloat16)


def product(x, y):
    dot = functools.partial(jnp.dot, preferred_element_type=jnp.float32)
    return dot(x[0], y[0]) + dot(x[0], y[1]) + dot(x[1], y[0])


def solve_kernel(sizes, loads, first, second, inverses, *refs):
    count = len(sizes)
    solved, (high, low, far_high, far_low, partial, x1, y2, d1, d2) = refs[:2], refs[2:11]
    x2, y1 = refs[11:11 + count], refs[11 + count:11 + 2 * count]
    (inv, rhs, top, part, swapped, passed, block, high_stage, low_stage,
     split_high, split_low,
     local_sem, link_send, link_recv, sum_send, sum_recv) = refs[11 + 2 * count:]
    r, c = lax.axis_index("row"), lax.axis_index("col")
    z, core = r // 2, lax.rem(r, 2)
    chips = inv.shape[1] // inv.shape[2] // 2
    rows = inv.shape[2]
    width = first.shape[2]
    x_side = c + 1 - 2 * lax.rem(c, 2)
    y_side = lax.rem(c + 2, 4)
    x_to, y_to = (r, x_side), (r, y_side)
    core_to = (r + 1 - 2 * core, c)

    def z_place(d):
        return lax.rem(z + d + chips, chips)

    def z_to(d):
        return (z_place(d) * 2 + core, c)

    def remote(src, dst, sends, recvs, at, to):
        return pltpu.make_async_remote_copy(src, dst, sends.at[at], recvs.at[at], device_id=to, device_id_type=MESH)

    inv_in = pltpu.make_async_copy(inverses, inv, local_sem.at[0])
    rhs_in = pltpu.make_async_copy(loads.at[pl.ds(0, 2)], rhs, local_sem.at[1])
    top_in = pltpu.make_async_copy(first.at[0], top.at[c], local_sem.at[2])
    inv_in.start()
    rhs_in.start()
    top_in.start()

    barrier = pltpu.get_barrier_semaphore()
    partners = [x_to, y_to, core_to] + [z_to(d) for d in range(1, chips)]
    for to in partners:
        pl.semaphore_signal(barrier, inc=1, device_id=to, device_id_type=MESH)
    pl.semaphore_wait(barrier, len(partners))

    top_in.wait()
    link = functools.partial(remote, sends=link_send, recvs=link_recv)
    top_x = link(top.at[c], top.at[c], at=0, to=x_to)
    top_y = link(top.at[c], top.at[c], at=1, to=y_to)
    top_d = link(top.at[y_side], top.at[y_side], at=2, to=x_to)
    send_d1 = link(y1[0], d1, at=3, to=x_to)
    send_d2 = link(x2[0], d2, at=4, to=y_to)
    starts = [sum(sizes[:k]) for k in range(count)]
    owned, send_x2, send_y1, send_x1, send_y2 = [], [], [], [], []
    for k, (start, size) in enumerate(zip(starts, sizes)):
        own1, own2 = first.at[pl.ds(start + 1, size)], second.at[pl.ds(start, size)]
        owned.append((own1, own2))
        send_x2.append(link(own2, x2[k], at=5 + 4 * k, to=x_to))
        send_y1.append(link(own1, y1[k], at=6 + 4 * k, to=y_to))
        send_x1.append(link(own1, x1.at[pl.ds(start, size)], at=7 + 4 * k, to=x_to))
        send_y2.append(link(own2, y2.at[pl.ds(start, size)], at=8 + 4 * k, to=y_to))
    for copy in (top_x, top_y, send_x2[0], send_y1[0]):
        copy.start()

    def top_recv(q, at):
        link(top.at[q], top.at[q], at=at, to=x_to).wait_recv()

    def finish(j, before, between):
        base = j * (4 * chips)
        at = functools.partial(remote, sends=sum_send, recvs=sum_recv)
        away = at(part.at[j, pl.ds((1 - core) * chips, chips)], swapped.at[j], at=base, to=core_to)
        away.start()
        before()
        away.wait_recv()

        @pl.loop(0, chips)
        def _(i):
            part[j, core * chips + i] += swapped[j, i]

        out = []
        for d in range(1, chips):
            copy = at(part.at[j, core * chips + z_place(d)], passed.at[j, d - 1], at=base + d, to=z_to(d))
            copy.start()
            out.append(copy)
        between()
        for copy in out:
            copy.wait_recv()
        mine = pl.ds(pl.multiple_of(r * rows, rows), rows)
        total = part[j, core * chips + z]
        for d in range(1, chips):
            total = total + passed[j, d - 1]
        block[j, mine] = total
        gathered = []
        for d in range(1, chips):
            copy = at(block.at[j, mine], block.at[j, mine], at=base + chips - 1 + d, to=z_to(d))
            copy.start()
            gathered.append(copy)
        across = [at(block.at[j, mine], block.at[j, mine], at=base + 2 * chips - 1, to=core_to)]
        across[0].start()
        return away, out, gathered, across, base, at

    def complete(j, state):
        away, out, gathered, across, base, at = state
        for d in range(1, chips):
            here = pl.ds(pl.multiple_of((z_place(-d) * 2 + core) * rows, rows), rows)
            at(block.at[j, here], block.at[j, here], at=base + chips - 1 + d, to=z_to(d)).wait_recv()
            copy = at(block.at[j, here], block.at[j, here], at=base + 2 * chips - 1 + d, to=core_to)
            copy.start()
            across.append(copy)
        for d in range(chips):
            there = pl.ds(pl.multiple_of((z_place(-d) * 2 + 1 - core) * rows, rows), rows)
            at(block.at[j, there], block.at[j, there], at=base + 2 * chips - 1 + d, to=core_to).wait_recv()
        for copy in [away] + out + gathered + across:
            copy.wait_send()

    def term(j, right):
        @pl.loop(0, 2 * chips)
        def _(i):
            owner = lax.rem(i, chips) * 2 + i // chips
            left = inv[j, pl.ds(pl.multiple_of(owner * rows, rows), rows)]
            part[j, i] = product(halves(left), right)

    def stage(j):
        for k, q in enumerate((c, x_side, y_side, 3 - c)):
            quarter = block[j, pl.ds(pl.multiple_of(q * width, width), width)]
            h, l = halves(quarter)
            high_stage[j, k * width:(k + 1) * width] = h
            low_stage[j, k * width:(k + 1) * width] = l
        near, here, whole = 3 * width, pl.ds(j * width, width), pl.ds(j * 4 * width, 4 * width)
        moves = [
            (block.at[j], solved[j]),
            (high_stage.at[j], high.at[whole]),
            (low_stage.at[j], low.at[whole]),
            (high_stage.at[j, pl.ds(near, width)], far_high.at[here]),
            (low_stage.at[j, pl.ds(near, width)], far_low.at[here]),
        ]
        copies = [pltpu.make_async_copy(src, dst, local_sem.at[3 + 5 * j + k]) for k, (src, dst) in enumerate(moves)]
        for copy in copies:
            copy.start()
        return copies

    inv_in.wait()
    rhs_in.wait()
    term(0, halves(rhs[0]))

    def forward_top():
        top_recv(y_side, 1)
        top_d.start()
        send_x1[0].start()
        send_y2[0].start()

    def queue_rest():
        for k in range(1, count):
            for copy in (send_x2[k], send_y1[k], send_x1[k], send_y2[k]):
                copy.start()

    def forward_first():
        send_y1[0].wait_recv()
        send_d1.start()
        send_x2[0].wait_recv()
        send_d2.start()

    def nothing():
        pass

    state = finish(0, forward_top, queue_rest)
    complete(0, state)
    copies = stage(0)
    top_recv(x_side, 0)
    top_recv(3 - c, 2)
    update = rhs[1]
    for q in range(4):
        left = halves(top[q])
        right = halves(block[0, q * width:(q + 1) * width])
        update = update - product(left, right)
    term(1, halves(update))

    state = finish(1, nothing, forward_first)
    complete(1, state)
    copies += stage(1)

    near = 3 * width

    def step_body(*views):
        loads_view, out_view = views[6:]
        for at, piece in enumerate(views[:6]):
            h, l = halves(piece[...].reshape(STEP * rows, width))
            split_high[:, at * width:(at + 1) * width] = h
            split_low[:, at * width:(at + 1) * width] = l
        total = product((split_high[:, :near], split_low[:, :near]), (high_stage[0, :near], low_stage[0, :near]))
        total = total + product((split_high[:, near:], split_low[:, near:]), (high_stage[1, :near], low_stage[1, :near]))
        out_view[...] = loads_view[...] - total.reshape(STEP, rows, total.shape[1])

    columns = rhs.shape[2]
    narrow = pl.BlockSpec((STEP, rows, width), lambda i: (i, 0, 0))
    wide = pl.BlockSpec((STEP, rows, columns), lambda i: (i, 0, 0))
    for k, (start, size) in enumerate(zip(starts, sizes)):
        here = pl.ds(start, size)
        for copy in (send_x1[k], send_y2[k]) + ((send_x2[k], send_y1[k]) if k else ()):
            copy.wait_recv()
        if k == 0:
            continue
        pltpu.emit_pipeline(step_body, grid=(size // STEP,), in_specs=[narrow] * 6 + [wide], out_specs=[wide])(
            owned[k][0], x1.at[here], y1[k], owned[k][1], x2[k], y2.at[here],
            loads.at[pl.ds(start + 2, size)], partial.at[here])
    for copy in copies:
        copy.wait()
    for copy in [top_x, top_y, top_d] + send_x1 + send_y1 + send_x2 + send_y2:
        copy.wait_send()
    for copy in (send_d1, send_d2):
        copy.wait()


def solve(sizes, row_count, loads, first, second, inverses):
    chips = row_count // 2
    rows, columns = loads.shape[1:]
    width = first.shape[2]
    depth = 4 * width
    f32, bf16 = jnp.float32, jnp.bfloat16
    anywhere = pl.BlockSpec(memory_space=pl.ANY)
    shape = jax.ShapeDtypeStruct
    piece = lambda size: shape((size, rows, width), f32)
    pieces = [piece(size) for size in [sum(sizes)] * 2 + [sizes[0]] * 2 + list(sizes) * 2]
    links = 5 + 4 * len(sizes)
    sums = 2 * 4 * chips
    return pl.pallas_call(
        functools.partial(solve_kernel, sizes),
        out_shape=[shape((depth, columns), f32)] * 2 + [shape((2 * depth, columns), bf16)] * 2
        + [shape((2 * width, columns), bf16)] * 2
        + [shape((sum(sizes), rows, columns), f32)] + pieces,
        in_specs=[anywhere] * 4,
        out_specs=[anywhere] * (7 + len(pieces)),
        scratch_shapes=[
            pltpu.VMEM((2, depth, rows), f32),
            pltpu.VMEM((2, rows, columns), f32),
            pltpu.VMEM((4, rows, width), f32),
            pltpu.VMEM((2, 2 * chips, rows, columns), f32),
            pltpu.VMEM((2, chips, rows, columns), f32),
            pltpu.VMEM((2, chips - 1, rows, columns), f32),
            pltpu.VMEM((2, depth, columns), f32),
            pltpu.VMEM((2, depth, columns), bf16),
            pltpu.VMEM((2, depth, columns), bf16),
            pltpu.VMEM((STEP * rows, 6 * width), bf16),
            pltpu.VMEM((STEP * rows, 6 * width), bf16),
            pltpu.SemaphoreType.DMA((13,)),
            pltpu.SemaphoreType.DMA((links,)),
            pltpu.SemaphoreType.DMA((links,)),
            pltpu.SemaphoreType.DMA((sums,)),
            pltpu.SemaphoreType.DMA((sums,)),
        ],
        compiler_params=pltpu.CompilerParams(
            collective_id=0, has_side_effects=True, vmem_limit_bytes=60 * 1024 * 1024,
        ),
    )(loads, first, second, inverses)


def update_kernel(count, step, *refs):
    pieces = refs[:count]
    loads = refs[count:count + step // 2]
    high_ref, low_ref = refs[count + step // 2:count + step // 2 + 2]
    out, ah, al = refs[-3:]
    rows, width = pieces[0].shape[1:]
    for at, piece in enumerate(pieces):
        high, low = halves(piece[...].reshape(step * rows, width))
        ah[:, at * width:(at + 1) * width] = high
        al[:, at * width:(at + 1) * width] = low
    total = product((ah[...], al[...]), (high_ref[...], low_ref[...]))
    total = total.reshape(step, rows, total.shape[1])
    for at, part in enumerate(loads):
        out[2 * at:2 * at + 2] = part[...] - total[2 * at:2 * at + 2]


def update_chunk(pieces, loads, skip, high, low, offset, size, previous):
    rows, width = pieces[0][0].shape[1:]
    columns = loads.shape[2]
    depth = high.shape[0]
    count = loads.shape[0] - skip
    step = STEPS if size % STEPS == 0 and offset % STEPS == 0 else 2
    operands, in_specs = [], []
    for array, at in pieces:
        operands.append(array)
        in_specs.append(pl.BlockSpec(
            (pl.Element(step), pl.Element(rows), pl.Element(width)),
            lambda i, at=at: (at + i * step, 0, 0)))
    for k in range(step // 2):
        operands.append(loads)
        in_specs.append(pl.BlockSpec((2, rows, columns), lambda i, k=k: ((skip + offset + i * step) // 2 + k, 0, 0)))
    for factor in (high, low):
        operands.append(factor)
        in_specs.append(pl.BlockSpec((depth, columns), lambda i: (0, 0), pipeline_mode=pl.Buffered(1)))
    aliases = {}
    if previous is not None:
        aliases = {len(operands): 0}
        operands.append(previous)
        in_specs.append(pl.BlockSpec(memory_space=pl.ANY))
    work = size * rows * depth * columns
    return pl.pallas_call(
        functools.partial(update_kernel, len(pieces), step),
        out_shape=jax.ShapeDtypeStruct((count, rows, columns), jnp.float32),
        grid=(size // step,),
        in_specs=in_specs,
        out_specs=pl.BlockSpec((step, rows, columns), lambda i: (offset // step + i, 0, 0)),
        scratch_shapes=[pltpu.VMEM((step * rows, depth), jnp.bfloat16)] * 2,
        input_output_aliases=aliases,
        compiler_params=pltpu.CompilerParams(vmem_limit_bytes=60 * 1024 * 1024),
        cost_estimate=pl.CostEstimate(
            flops=6 * work,
            bytes_accessed=4 * size * rows * (depth + 2 * columns) + 4 * depth * columns,
            transcendentals=0,
        ),
    )(*operands)


def local_quarters(row_count, loads, below_first, below_second, inverses):
    sizes = chunk_sizes(loads.shape[0] - 2)
    along_x = [(c, c ^ 1) for c in range(4)]
    along_y = [(c, c ^ 2) for c in range(4)]
    results = solve(sizes, row_count, loads, below_first, below_second, inverses)
    solved, (high, low, far_high, far_low, partial, x1, y2, d1, d2) = results[:2], results[2:11]
    x2, y1 = results[11:11 + len(sizes)], results[11 + len(sizes):]
    pieces = [(below_first, 1), (x1, 0), (y1[0], 0), (d1, 0), (below_second, 0), (x2[0], 0), (y2, 0), (d2, 0)]
    remaining = update_chunk(pieces, loads, 2, high, low, 0, sizes[0], None)
    solved, far_high = lax.optimization_barrier((jnp.stack(solved), far_high))
    far1, far2 = {}, {}
    for k in range(1, len(sizes)):
        near1, near2 = y1[k], x2[k]
        if k > 2:
            near1, far1[k - 2] = lax.optimization_barrier((near1, far1[k - 2]))
            near2, far2[k - 2] = lax.optimization_barrier((near2, far2[k - 2]))
        far1[k] = lax.ppermute(near1, "col", along_x)
        far2[k] = lax.ppermute(near2, "col", along_y)
    at = sizes[0]
    for k in range(1, len(sizes)):
        chunk = [(far1[k], 0), (far2[k], 0)]
        remaining = update_chunk(chunk, partial, 0, far_high, far_low, at, sizes[k], remaining)
        at += sizes[k]
    return solved, remaining


def local_gathered(loads, below_first, below_second, inverses):
    count = loads.shape[0] - 2
    gather = lambda piece: lax.all_gather(piece, "col", axis=2, tiled=True)
    top = gather(below_first[:1])
    first_block = lax.psum(jnp.dot(inverses[0], loads[0], precision=HIGH), "row")
    updated = loads[1] - jnp.dot(top[0], first_block, precision=HIGH)
    second_block = lax.psum(jnp.dot(inverses[1], updated, precision=HIGH), "row")
    solved = jnp.stack([first_block, second_block])
    whole = solved.reshape(-1, solved.shape[2])
    high = lax.reduce_precision(whole, 8, 7)
    high, low = high.astype(jnp.bfloat16), (whole - high).astype(jnp.bfloat16)
    remaining = None
    at = 0
    for size in (count // 8 * 4, count - count // 8 * 4):
        pieces = [(gather(below_first[at + 1:at + 1 + size]), 0), (gather(below_second[at:at + size]), 0)]
        remaining = update_chunk(pieces, loads, 2, high, low, at, size, remaining)
        at += size
    return solved, remaining


def solution(mesh):
    in_specs = (
        P(None, "row", "col"),
        P(None, "row", "col"),
        P(None, "row", "col"),
        P(None, None, "row"),
    )
    out_specs = (P(None, None, "col"), P(None, "row", "col"))
    quarters = mesh.shape["col"] == 4 and mesh.shape["row"] % 2 == 0
    local = functools.partial(local_quarters, mesh.shape["row"]) if quarters else local_gathered
    return jax.shard_map(local, mesh=mesh, in_specs=in_specs, out_specs=out_specs, check_vma=False)
```

```python
import functools
import jax
import jax.numpy as jnp
from jax import lax
from jax.experimental import pallas as pl
from jax.experimental.pallas import tpu as pltpu
from jax.sharding import PartitionSpec as P

HIGH = lax.Precision.HIGH
MESH = pl.DeviceIdType.MESH
STEP = 2
STEPS = 4


def chunk_sizes(count):
    first, last = count // 10 * 2, count // 20 * 2
    middle = count - first - last
    parts = -(-middle // 12)
    at = [k * middle // (2 * parts) * 2 for k in range(parts)] + [middle]
    return [first] + [after - before for before, after in zip(at, at[1:])] + [last]


def halves(value):
    high = value.astype(jnp.bfloat16)
    return high, (value - high.astype(jnp.float32)).astype(jnp.bfloat16)


def product(x, y):
    dot = functools.partial(jnp.dot, preferred_element_type=jnp.float32)
    return dot(x[0], y[0]) + dot(x[0], y[1]) + dot(x[1], y[0])


def solve_kernel(sizes, loads, first, second, inverses, *refs):
    count = len(sizes)
    solved, (high, low, far_high, far_low, partial, x1, y2, d1, d2) = refs[:2], refs[2:11]
    x2, y1 = refs[11:11 + count], refs[11 + count:11 + 2 * count]
    (inv, rhs, top, part, swapped, passed, block, high_stage, low_stage,
     split_high, split_low,
     local_sem, link_send, link_recv, sum_send, sum_recv) = refs[11 + 2 * count:]
    r, c = lax.axis_index("row"), lax.axis_index("col")
    z, core = r // 2, lax.rem(r, 2)
    chips = inv.shape[1] // inv.shape[2] // 2
    rows = inv.shape[2]
    width = first.shape[2]
    x_side = c + 1 - 2 * lax.rem(c, 2)
    y_side = lax.rem(c + 2, 4)
    x_to, y_to = (r, x_side), (r, y_side)
    core_to = (r + 1 - 2 * core, c)

    def z_place(d):
        return lax.rem(z + d + chips, chips)

    def z_to(d):
        return (z_place(d) * 2 + core, c)

    def remote(src, dst, sends, recvs, at, to):
        return pltpu.make_async_remote_copy(src, dst, sends.at[at], recvs.at[at], device_id=to, device_id_type=MESH)

    inv_in = pltpu.make_async_copy(inverses, inv, local_sem.at[0])
    rhs_in = pltpu.make_async_copy(loads.at[pl.ds(0, 2)], rhs, local_sem.at[1])
    top_in = pltpu.make_async_copy(first.at[0], top.at[c], local_sem.at[2])
    inv_in.start()
    rhs_in.start()
    top_in.start()

    barrier = pltpu.get_barrier_semaphore()
    partners = [x_to, y_to, core_to] + [z_to(d) for d in range(1, chips)]
    for to in partners:
        pl.semaphore_signal(barrier, inc=1, device_id=to, device_id_type=MESH)
    pl.semaphore_wait(barrier, len(partners))

    link = functools.partial(remote, sends=link_send, recvs=link_recv)
    upper, lower = pl.ds(0, rows // 2), pl.ds(rows // 2, rows - rows // 2)
    last_link = 5 + 4 * count
    top_x = link(first.at[0], top.at[c], at=0, to=x_to)
    top_y = link(first.at[0], top.at[c], at=1, to=y_to)
    top_d1 = link(top.at[y_side, upper], top.at[y_side, upper], at=2, to=x_to)
    top_d2 = link(top.at[x_side, lower], top.at[x_side, lower], at=last_link, to=y_to)
    send_d1 = link(y1[0], d1, at=3, to=x_to)
    send_d2 = link(x2[0], d2, at=4, to=y_to)
    starts = [sum(sizes[:k]) for k in range(count)]
    owned, send_x2, send_y1, send_x1, send_y2 = [], [], [], [], []
    for k, (start, size) in enumerate(zip(starts, sizes)):
        own1, own2 = first.at[pl.ds(start + 1, size)], second.at[pl.ds(start, size)]
        owned.append((own1, own2))
        send_x2.append(link(own2, x2[k], at=5 + 4 * k, to=x_to))
        send_y1.append(link(own1, y1[k], at=6 + 4 * k, to=y_to))
        send_x1.append(link(own1, x1.at[pl.ds(start, size)], at=7 + 4 * k, to=x_to))
        send_y2.append(link(own2, y2.at[pl.ds(start, size)], at=8 + 4 * k, to=y_to))
    for copy in (top_x, top_y, send_x2[0], send_y1[0]):
        copy.start()

    def top_recv(q, at):
        link(top.at[q], top.at[q], at=at, to=x_to).wait_recv()

    def finish(j, before, between):
        base = j * (4 * chips)
        at = functools.partial(remote, sends=sum_send, recvs=sum_recv)
        away = at(part.at[j, pl.ds((1 - core) * chips, chips)], swapped.at[j], at=base, to=core_to)
        away.start()
        before()
        away.wait_recv()

        @pl.loop(0, chips)
        def _(i):
            part[j, core * chips + i] += swapped[j, i]

        out = []
        for d in range(1, chips):
            copy = at(part.at[j, core * chips + z_place(d)], passed.at[j, d - 1], at=base + d, to=z_to(d))
            copy.start()
            out.append(copy)
        between()
        for copy in out:
            copy.wait_recv()
        mine = pl.ds(pl.multiple_of(r * rows, rows), rows)
        total = part[j, core * chips + z]
        for d in range(1, chips):
            total = total + passed[j, d - 1]
        block[j, mine] = total
        gathered = []
        for d in range(1, chips):
            copy = at(block.at[j, mine], block.at[j, mine], at=base + chips - 1 + d, to=z_to(d))
            copy.start()
            gathered.append(copy)
        across = [at(block.at[j, mine], block.at[j, mine], at=base + 2 * chips - 1, to=core_to)]
        across[0].start()
        return away, out, gathered, across, base, at

    def complete(j, state):
        away, out, gathered, across, base, at = state
        for d in range(1, chips):
            here = pl.ds(pl.multiple_of((z_place(-d) * 2 + core) * rows, rows), rows)
            at(block.at[j, here], block.at[j, here], at=base + chips - 1 + d, to=z_to(d)).wait_recv()
            copy = at(block.at[j, here], block.at[j, here], at=base + 2 * chips - 1 + d, to=core_to)
            copy.start()
            across.append(copy)
        for d in range(chips):
            there = pl.ds(pl.multiple_of((z_place(-d) * 2 + 1 - core) * rows, rows), rows)
            at(block.at[j, there], block.at[j, there], at=base + 2 * chips - 1 + d, to=core_to).wait_recv()
        for copy in [away] + out + gathered + across:
            copy.wait_send()

    def term(j, right):
        @pl.loop(0, 2 * chips)
        def _(i):
            owner = lax.rem(i, chips) * 2 + i // chips
            left = inv[j, pl.ds(pl.multiple_of(owner * rows, rows), rows)]
            part[j, i] = product(halves(left), right)

    def stage(j):
        for k, q in enumerate((c, x_side, y_side, 3 - c)):
            quarter = block[j, pl.ds(pl.multiple_of(q * width, width), width)]
            h, l = halves(quarter)
            high_stage[j, k * width:(k + 1) * width] = h
            low_stage[j, k * width:(k + 1) * width] = l
        near, here, whole = 3 * width, pl.ds(j * width, width), pl.ds(j * 4 * width, 4 * width)
        moves = [
            (block.at[j], solved[j]),
            (high_stage.at[j], high.at[whole]),
            (low_stage.at[j], low.at[whole]),
            (high_stage.at[j, pl.ds(near, width)], far_high.at[here]),
            (low_stage.at[j, pl.ds(near, width)], far_low.at[here]),
        ]
        copies = [pltpu.make_async_copy(src, dst, local_sem.at[3 + 5 * j + k]) for k, (src, dst) in enumerate(moves)]
        for copy in copies:
            copy.start()
        return copies

    inv_in.wait()
    rhs_in.wait()
    term(0, halves(rhs[0]))

    def forward_top():
        top_recv(y_side, 1)
        top_d1.start()
        top_recv(x_side, 0)
        top_d2.start()
        send_x1[0].start()
        send_y2[0].start()

    def queue_rest():
        for k in range(1, count):
            for copy in (send_x2[k], send_y1[k], send_x1[k], send_y2[k]):
                copy.start()

    def forward_first():
        send_y1[0].wait_recv()
        send_d1.start()
        send_x2[0].wait_recv()
        send_d2.start()

    def nothing():
        pass

    state = finish(0, forward_top, queue_rest)
    complete(0, state)
    copies = stage(0)
    top_in.wait()
    for half, at in ((upper, 2), (lower, last_link)):
        link(top.at[3 - c, half], top.at[3 - c, half], at=at, to=x_to).wait_recv()
    update = rhs[1]
    for q in range(4):
        left = halves(top[q])
        right = halves(block[0, q * width:(q + 1) * width])
        update = update - product(left, right)
    term(1, halves(update))

    state = finish(1, nothing, forward_first)
    complete(1, state)
    copies += stage(1)

    near = 3 * width

    def step_body(*views):
        loads_view, out_view = views[6:]
        for at, piece in enumerate(views[:6]):
            h, l = halves(piece[...].reshape(STEP * rows, width))
            split_high[:, at * width:(at + 1) * width] = h
            split_low[:, at * width:(at + 1) * width] = l
        total = product((split_high[:, :near], split_low[:, :near]), (high_stage[0, :near], low_stage[0, :near]))
        total = total + product((split_high[:, near:], split_low[:, near:]), (high_stage[1, :near], low_stage[1, :near]))
        out_view[...] = loads_view[...] - total.reshape(STEP, rows, total.shape[1])

    columns = rhs.shape[2]
    narrow = pl.BlockSpec((STEP, rows, width), lambda i: (i, 0, 0))
    wide = pl.BlockSpec((STEP, rows, columns), lambda i: (i, 0, 0))
    for k, (start, size) in enumerate(zip(starts, sizes)):
        here = pl.ds(start, size)
        for copy in (send_x1[k], send_y2[k]) + ((send_x2[k], send_y1[k]) if k else ()):
            copy.wait_recv()
        if k == 0:
            continue
        pltpu.emit_pipeline(step_body, grid=(size // STEP,), in_specs=[narrow] * 6 + [wide], out_specs=[wide])(
            owned[k][0], x1.at[here], y1[k], owned[k][1], x2[k], y2.at[here],
            loads.at[pl.ds(start + 2, size)], partial.at[here])
    for copy in copies:
        copy.wait()
    for copy in [top_x, top_y, top_d1, top_d2] + send_x1 + send_y1 + send_x2 + send_y2:
        copy.wait_send()
    for copy in (send_d1, send_d2):
        copy.wait()


def solve(sizes, row_count, loads, first, second, inverses):
    chips = row_count // 2
    rows, columns = loads.shape[1:]
    width = first.shape[2]
    depth = 4 * width
    f32, bf16 = jnp.float32, jnp.bfloat16
    anywhere = pl.BlockSpec(memory_space=pl.ANY)
    shape = jax.ShapeDtypeStruct
    piece = lambda size: shape((size, rows, width), f32)
    pieces = [piece(size) for size in [sum(sizes)] * 2 + [sizes[0]] * 2 + list(sizes) * 2]
    links = 6 + 4 * len(sizes)
    sums = 2 * 4 * chips
    return pl.pallas_call(
        functools.partial(solve_kernel, sizes),
        out_shape=[shape((depth, columns), f32)] * 2 + [shape((2 * depth, columns), bf16)] * 2
        + [shape((2 * width, columns), bf16)] * 2
        + [shape((sum(sizes), rows, columns), f32)] + pieces,
        in_specs=[anywhere] * 4,
        out_specs=[anywhere] * (7 + len(pieces)),
        scratch_shapes=[
            pltpu.VMEM((2, depth, rows), f32),
            pltpu.VMEM((2, rows, columns), f32),
            pltpu.VMEM((4, rows, width), f32),
            pltpu.VMEM((2, 2 * chips, rows, columns), f32),
            pltpu.VMEM((2, chips, rows, columns), f32),
            pltpu.VMEM((2, chips - 1, rows, columns), f32),
            pltpu.VMEM((2, depth, columns), f32),
            pltpu.VMEM((2, depth, columns), bf16),
            pltpu.VMEM((2, depth, columns), bf16),
            pltpu.VMEM((STEP * rows, 6 * width), bf16),
            pltpu.VMEM((STEP * rows, 6 * width), bf16),
            pltpu.SemaphoreType.DMA((13,)),
            pltpu.SemaphoreType.DMA((links,)),
            pltpu.SemaphoreType.DMA((links,)),
            pltpu.SemaphoreType.DMA((sums,)),
            pltpu.SemaphoreType.DMA((sums,)),
        ],
        compiler_params=pltpu.CompilerParams(
            collective_id=0, has_side_effects=True, vmem_limit_bytes=60 * 1024 * 1024,
        ),
    )(loads, first, second, inverses)


def update_kernel(count, step, *refs):
    pieces = refs[:count]
    loads = refs[count:count + step // 2]
    high_ref, low_ref = refs[count + step // 2:count + step // 2 + 2]
    out, ah, al = refs[-3:]
    rows, width = pieces[0].shape[1:]
    for at, piece in enumerate(pieces):
        high, low = halves(piece[...].reshape(step * rows, width))
        ah[:, at * width:(at + 1) * width] = high
        al[:, at * width:(at + 1) * width] = low
    total = product((ah[...], al[...]), (high_ref[...], low_ref[...]))
    total = total.reshape(step, rows, total.shape[1])
    for at, part in enumerate(loads):
        out[2 * at:2 * at + 2] = part[...] - total[2 * at:2 * at + 2]


def update_chunk(pieces, loads, skip, high, low, offset, size, previous):
    rows, width = pieces[0][0].shape[1:]
    columns = loads.shape[2]
    depth = high.shape[0]
    count = loads.shape[0] - skip
    step = STEPS if size % STEPS == 0 and offset % STEPS == 0 else 2
    operands, in_specs = [], []
    for array, at in pieces:
        operands.append(array)
        in_specs.append(pl.BlockSpec(
            (pl.Element(step), pl.Element(rows), pl.Element(width)),
            lambda i, at=at: (at + i * step, 0, 0)))
    for k in range(step // 2):
        operands.append(loads)
        in_specs.append(pl.BlockSpec((2, rows, columns), lambda i, k=k: ((skip + offset + i * step) // 2 + k, 0, 0)))
    for factor in (high, low):
        operands.append(factor)
        in_specs.append(pl.BlockSpec((depth, columns), lambda i: (0, 0), pipeline_mode=pl.Buffered(1)))
    aliases = {}
    if previous is not None:
        aliases = {len(operands): 0}
        operands.append(previous)
        in_specs.append(pl.BlockSpec(memory_space=pl.ANY))
    work = size * rows * depth * columns
    return pl.pallas_call(
        functools.partial(update_kernel, len(pieces), step),
        out_shape=jax.ShapeDtypeStruct((count, rows, columns), jnp.float32),
        grid=(size // step,),
        in_specs=in_specs,
        out_specs=pl.BlockSpec((step, rows, columns), lambda i: (offset // step + i, 0, 0)),
        scratch_shapes=[pltpu.VMEM((step * rows, depth), jnp.bfloat16)] * 2,
        input_output_aliases=aliases,
        compiler_params=pltpu.CompilerParams(vmem_limit_bytes=60 * 1024 * 1024),
        cost_estimate=pl.CostEstimate(
            flops=6 * work,
            bytes_accessed=4 * size * rows * (depth + 2 * columns) + 4 * depth * columns,
            transcendentals=0,
        ),
    )(*operands)


def local_quarters(row_count, loads, below_first, below_second, inverses):
    sizes = chunk_sizes(loads.shape[0] - 2)
    along_x = [(c, c ^ 1) for c in range(4)]
    along_y = [(c, c ^ 2) for c in range(4)]
    results = solve(sizes, row_count, loads, below_first, below_second, inverses)
    solved, (high, low, far_high, far_low, partial, x1, y2, d1, d2) = results[:2], results[2:11]
    x2, y1 = results[11:11 + len(sizes)], results[11 + len(sizes):]
    pieces = [(below_first, 1), (x1, 0), (y1[0], 0), (d1, 0), (below_second, 0), (x2[0], 0), (y2, 0), (d2, 0)]
    remaining = update_chunk(pieces, loads, 2, high, low, 0, sizes[0], None)
    solved, far_high = lax.optimization_barrier((jnp.stack(solved), far_high))
    far1, far2 = {}, {}
    for k in range(1, len(sizes)):
        near1, near2 = y1[k], x2[k]
        if k > 2:
            near1, far1[k - 2] = lax.optimization_barrier((near1, far1[k - 2]))
            near2, far2[k - 2] = lax.optimization_barrier((near2, far2[k - 2]))
        far1[k] = lax.ppermute(near1, "col", along_x)
        far2[k] = lax.ppermute(near2, "col", along_y)
    at = sizes[0]
    for k in range(1, len(sizes)):
        chunk = [(far1[k], 0), (far2[k], 0)]
        remaining = update_chunk(chunk, partial, 0, far_high, far_low, at, sizes[k], remaining)
        at += sizes[k]
    return solved, remaining


def local_gathered(loads, below_first, below_second, inverses):
    count = loads.shape[0] - 2
    gather = lambda piece: lax.all_gather(piece, "col", axis=2, tiled=True)
    top = gather(below_first[:1])
    first_block = lax.psum(jnp.dot(inverses[0], loads[0], precision=HIGH), "row")
    updated = loads[1] - jnp.dot(top[0], first_block, precision=HIGH)
    second_block = lax.psum(jnp.dot(inverses[1], updated, precision=HIGH), "row")
    solved = jnp.stack([first_block, second_block])
    whole = solved.reshape(-1, solved.shape[2])
    high = lax.reduce_precision(whole, 8, 7)
    high, low = high.astype(jnp.bfloat16), (whole - high).astype(jnp.bfloat16)
    remaining = None
    at = 0
    for size in (count // 8 * 4, count - count // 8 * 4):
        pieces = [(gather(below_first[at + 1:at + 1 + size]), 0), (gather(below_second[at:at + size]), 0)]
        remaining = update_chunk(pieces, loads, 2, high, low, at, size, remaining)
        at += size
    return solved, remaining


def solution(mesh):
    in_specs = (
        P(None, "row", "col"),
        P(None, "row", "col"),
        P(None, "row", "col"),
        P(None, None, "row"),
    )
    out_specs = (P(None, None, "col"), P(None, "row", "col"))
    quarters = mesh.shape["col"] == 4 and mesh.shape["row"] % 2 == 0
    local = functools.partial(local_quarters, mesh.shape["row"]) if quarters else local_gathered
    return jax.shard_map(local, mesh=mesh, in_specs=in_specs, out_specs=out_specs, check_vma=False)
```
